32 devices in a mesh: draws: 2 (over x), spec: 16 (over z, y, core).
Axes of the slice: x: 2, y: 2, z: 4, core: 2. Of those that a mesh axis runs over, the one named last changes fastest.
Arguments:
- coefficients: bfloat16 [1280, 2, 320, 128], P('draws', None, 'spec'), parts along dimension 0, may hold values from -6 to 6
- legendre: float32 [640, 2, 320, 16], P('spec'), as said below
- row_counts: int32 [16], P('spec'), may hold values from 640 to 1280, as said below
- basis: float32 [64, 128], replicated, may hold values from -0.75 to 0.75
- absorb: float32 [128], replicated, may hold values from 0.00390625 to 0.0625
- peak_level: int32 [512], replicated, may hold values from 0 to 127
- width: float32 [512], replicated, may hold values from 1.5 to 12
Outputs:
- radiance: float32 [32, 2, 1280, 512], P(('draws', 'spec')), parts along dimension 0
The draws below stay inside these ranges and needn't reach their ends.
There are 2 independent parts, one for each index of `draws`. The reference program is written for one: setup_inputs(seed, part) draws one part's arguments, and reference() takes and returns one part's arrays. A program takes and returns all parts, laid end to end along the dimension named above; an argument that names none is the same for every part. Nothing has to cross between parts.
Inputs may be any that keep to these rules, and one draw needn't show every extreme that they name: `legendre`: entry [m, p, s, j] is the associated Legendre function of order m and degree m + 2 s + p, normalised to unit square integral over [-1, 1], at the cosine of a drawn colatitude of row j in the northern hemisphere; it is zero where the degree exceeds 640 - 1. `row_counts`: every count is a multiple of 4; row 0 has 1280 longitudes and row 1 has 640.
All inputs are finite; a program needn't handle non-finite values.
Results may differ from the reference program's by a relative error of at most 0.0003.
Values sent between devices are 32-bit elements; how exact they have to be, the bound alone decides.
No kernel may reach another device: no remote copies, remote signals or barrier semaphores. Data moves between devices by JAX's collectives and lax.ppermute only.
A program may use at most 128 MiB of HBM per device.

```python
import math
import jax
import jax.numpy as jnp
from jax import lax

MW = 640
NE = 320
NLON = 1280
NCH = 512
LEV = 128
K = 64
PR = 16


def draw_legendre(key, part):
    jitter = jax.random.uniform(key, (PR,), jnp.float32)
    colatitude = 0.5 * math.pi * (jnp.arange(PR, dtype=jnp.float32) + 0.2 + 0.6 * jitter) / PR
    cosine = jnp.cos(colatitude)
    log_sine = jnp.log(jnp.sin(colatitude))
    orders = jnp.arange(MW, dtype=jnp.float32)
    growth = jnp.concatenate((jnp.zeros((1,), jnp.float32), 0.5 * jnp.log((2.0 * orders[1:] + 1.0) / (2.0 * orders[1:]))))
    log_start = 0.5 * math.log(0.5) + jnp.cumsum(growth)
    diagonal_start = jnp.exp(log_start[:, None] + orders[:, None] * log_sine[None, :])

    def advance(carry, offset):
        previous, current = carry
        degree = orders + offset
        below = degree - 1.0
        coupling_now = jnp.sqrt(jnp.maximum((degree * degree - orders * orders) / (4.0 * degree * degree - 1.0), 0.0))
        coupling_prev = jnp.sqrt(jnp.maximum((below * below - orders * orders) / (4.0 * below * below - 1.0), 0.0))
        following = (cosine[None, :] * current - coupling_prev[:, None] * previous) / coupling_now[:, None]
        return ((current, following), following)
    offsets = jnp.arange(1, MW, dtype=jnp.float32)
    carried, values = lax.scan(advance, (jnp.zeros_like(diagonal_start), diagonal_start), offsets)
    whole = jnp.concatenate((diagonal_start[None], values), axis=0)
    degree_offset = jnp.arange(MW, dtype=jnp.int32)[:, None, None]
    order_index = jnp.arange(MW, dtype=jnp.int32)[None, :, None]
    whole = jnp.where(degree_offset + order_index < MW, whole, jnp.zeros_like(whole))
    arranged = whole.reshape(MW // 2, 2, MW, PR)
    return jnp.transpose(arranged, (2, 1, 0, 3)).astype(jnp.float32)


def draw_row_counts(key, part):
    increments = jax.random.randint(key, (PR,), 0, NLON // 8 + 1)
    counts = NLON // 2 + 4 * increments
    counts = counts.at[0].set(NLON).at[1].set(NLON // 2)
    return counts.astype(jnp.int32)


def set_ends(values, rng, low, high):
    index_at = [jax.random.randint(jax.random.fold_in(rng, axis), (), 0, length) for axis, length in enumerate(values.shape)]
    main_axis = values.shape.index(max(values.shape))
    next_to = index_at[:main_axis] + [(index_at[main_axis] + 1) % values.shape[main_axis]] + index_at[main_axis + 1:]
    return values.at[tuple(index_at)].set(low).at[tuple(next_to)].set(high)


def shard_levels(own_key, extent, cuts, smallest, top_value):
    gain, own = 1.0, jax.random.fold_in(own_key, 6)
    for position, parts in cuts:
        draws = jnp.exp(jax.random.uniform(jax.random.fold_in(own, position), (parts,), jnp.float32, smallest / len(cuts), top_value / len(cuts)))
        gain = gain * jnp.repeat(draws, extent[position] // parts).reshape([-1 if axis == position else 1 for axis in range(len(extent))])
    return gain


def centred(own_key, extent, scale, most, cuts=(), kind=jnp.bfloat16):
    entries = scale * jax.random.normal(own_key, extent, jnp.float32)
    if cuts:
        entries = entries * shard_levels(own_key, extent, cuts, -0.22, 0.18)
    return jnp.clip(entries, -most, most).astype(kind)


def setup_inputs(seed: int = 0, part: int = 0) -> dict:
    streams_of = jax.random.split(jax.random.key(seed), 8)
    part_splits = jax.random.split(jax.random.fold_in(streams_of[7], part), 8)
    coefficients = centred(part_splits[0], (MW, 2, NE, 2 * K), 1.0, 6.0, ((2, 16),))
    legendre = draw_legendre(jax.random.fold_in(streams_of[7], 71), part)
    row_counts = draw_row_counts(jax.random.fold_in(streams_of[7], 71), part)
    basis = centred(streams_of[3], (K, LEV), K ** -0.5, 0.75, (), jnp.float32)
    absorb = jnp.clip(jnp.exp(jax.random.uniform(streams_of[4], (LEV,), jnp.float32, math.log(0.00390625), math.log(0.0625))), 0.00390625, 0.0625)
    peak_level = set_ends(jax.random.randint(streams_of[5], (NCH,), 0, LEV), jax.random.fold_in(streams_of[5], 1), 0, LEV - 1).astype(jnp.int32)
    width = jnp.clip(jnp.exp(jax.random.uniform(streams_of[6], (NCH,), jnp.float32, math.log(1.5), math.log(12.0))), 1.5, 12.0)
    return {"coefficients": coefficients, "legendre": legendre, "row_counts": row_counts, "basis": basis, "absorb": absorb, "peak_level": peak_level, "width": width}


PRECISE = lax.Precision.HIGHEST

def prior_scale(shard, first):
    waves = shard.shape[0]
    slots = shard.shape[2]
    orders = jnp.arange(waves, dtype=jnp.int32)[:, None, None]
    parity = jnp.arange(2, dtype=jnp.int32)[None, :, None]
    slot_index = first + jnp.arange(slots, dtype=jnp.int32)[None, None, :]
    degree = orders + 2 * slot_index + parity
    spread = lax.rsqrt((degree + 1).astype(jnp.float32) * waves)
    spread = jnp.where(degree < waves, spread, jnp.zeros_like(spread))
    return shard.astype(jnp.float32) * spread[..., None]

def expand_levels(values, modes_basis):
    lead = values.shape[:-1]
    halves = values.reshape(lead + (2, modes_basis.shape[0]))
    expanded = jnp.einsum('abcqk,kl->abcql', halves, modes_basis, precision=PRECISE)
    return expanded.reshape(lead + (2 * modes_basis.shape[1],))

def channel_kernel(peak_level, width, levels):
    height = jnp.arange(levels, dtype=jnp.float32)[:, None]
    offsets = (height - peak_level.astype(jnp.float32)[None, :]) / width[None, :]
    weights = jnp.exp(-offsets * offsets)
    return weights / lax.optimization_barrier(jnp.sum(weights, axis=0, keepdims=True))

def radiate(temps, absorb, kernel):
    levels = temps.shape[-1]
    strict_upper = (jnp.arange(levels)[:, None] < jnp.arange(levels)[None, :]).astype(jnp.float32)
    source = jnp.exp(0.5 * temps)
    layers = absorb[None, :] * source
    overhead = jnp.dot(layers, strict_upper, precision=PRECISE, preferred_element_type=jnp.float32)
    emitted = source * jnp.exp(-overhead) * -jnp.expm1(-layers)
    return jnp.dot(emitted, kernel, precision=PRECISE, preferred_element_type=jnp.float32)

def fourier_lookup(row_count, waves, points):
    orders = jnp.arange(waves, dtype=jnp.int32)
    places = jnp.arange(points, dtype=jnp.int32)
    phases = places[:, None] * orders[None, :] % row_count
    angles = 2.0 * math.pi * phases.astype(jnp.float32) / row_count.astype(jnp.float32)
    weights = jnp.where(orders == 0, 1.0, 2.0) * (2 * orders < row_count).astype(jnp.float32)
    return jnp.stack((weights * jnp.cos(angles), -weights * jnp.sin(angles)), axis=-1)

def synthesize_row(spectra, row_count, modes_basis, absorb, kernel, points):
    waves, hemis, columns = spectra.shape
    lookup = fourier_lookup(row_count, waves, points)
    split_parts = spectra.reshape(waves, hemis, 2, columns // 2)
    fields = jnp.einsum('kmq,mhqc->hkc', lookup, split_parts, precision=PRECISE)
    if modes_basis is not None:
        fields = jnp.einsum('hkc,cl->hkl', fields, modes_basis, precision=PRECISE)
    levels = fields.shape[-1]
    bright = radiate(fields.reshape(hemis * points, levels), absorb, kernel)
    bright = bright.reshape(hemis, points, kernel.shape[1])
    inside = (jnp.arange(points, dtype=jnp.int32) < row_count).astype(jnp.float32)
    return bright * inside[None, :, None]

def reference(coefficients, legendre, row_counts, basis, absorb, peak_level, width):
    scaled = prior_scale(coefficients, 0)
    spectral = expand_levels(scaled, basis)
    even_odd = jnp.einsum('mpsj,mpsc->mpjc', legendre, spectral, precision=PRECISE)
    fourier = jnp.stack((even_odd[:, 0] + even_odd[:, 1], even_odd[:, 0] - even_odd[:, 1]), axis=1)
    kernel = channel_kernel(peak_level, width, LEV)

    def one_row(inputs):
        spectra, row_count = inputs
        return synthesize_row(spectra, row_count, None, absorb, kernel, NLON)
    return lax.map(one_row, (jnp.moveaxis(fourier, 2, 0), row_counts))
```

```python
import functools
import math

import jax
import jax.numpy as jnp
from jax import lax
from jax.experimental import pallas as pl
from jax.experimental.pallas import tpu as pltpu
from jax.sharding import PartitionSpec as P

NLON = 1280
STEP = 32
PLANES = 4
PAD = 32

PRECISE = lax.Precision.HIGHEST
F32 = jnp.float32
BF16 = jnp.bfloat16


def prior_scale(shard, first):
    waves = shard.shape[0]
    slots = shard.shape[2]
    orders = jnp.arange(waves, dtype=jnp.int32)[:, None, None]
    parity = jnp.arange(2, dtype=jnp.int32)[None, :, None]
    slot_index = first + jnp.arange(slots, dtype=jnp.int32)[None, None, :]
    degree = orders + 2 * slot_index + parity
    spread = lax.rsqrt((degree + 1).astype(F32) * waves)
    spread = jnp.where(degree < waves, spread, jnp.zeros_like(spread))
    return shard.astype(F32) * spread[..., None]


def channel_kernel(peak_level, width, levels):
    height = jnp.arange(levels, dtype=F32)[:, None]
    offsets = (height - peak_level.astype(F32)[None, :]) / width[None, :]
    weights = jnp.exp(-offsets * offsets)
    return weights / jnp.sum(weights, axis=0, keepdims=True)


def radiate(temps, absorb, kernel):
    levels = temps.shape[-1]
    strict_upper = (jnp.arange(levels)[:, None] < jnp.arange(levels)[None, :]).astype(F32)
    source = jnp.exp(0.5 * temps)
    layers = absorb[None, :] * source
    overhead = jnp.dot(layers, strict_upper, precision=PRECISE, preferred_element_type=F32)
    emitted = source * jnp.exp(-overhead) * -jnp.expm1(-layers)
    return jnp.dot(emitted, kernel, precision=PRECISE, preferred_element_type=F32)


def fourier_lookup(row_count, waves, points):
    orders = jnp.arange(waves, dtype=jnp.int32)
    places = jnp.arange(points, dtype=jnp.int32)
    phases = places[:, None] * orders[None, :] % row_count
    angles = 2.0 * math.pi * phases.astype(F32) / row_count.astype(F32)
    weights = jnp.where(orders == 0, 1.0, 2.0) * (2 * orders < row_count).astype(F32)
    return jnp.stack((weights * jnp.cos(angles), -weights * jnp.sin(angles)), axis=-1)


def synthesize_row(spectra, row_count, modes_basis, absorb, kernel, points):
    waves, hemis, columns = spectra.shape
    lookup = fourier_lookup(row_count, waves, points)
    split_parts = spectra.reshape(waves, hemis, 2, columns // 2)
    fields = jnp.einsum("kmq,mhqc->hkc", lookup, split_parts, precision=PRECISE)
    fields = jnp.einsum("hkc,cl->hkl", fields, modes_basis, precision=PRECISE)
    levels = fields.shape[-1]
    bright = radiate(fields.reshape(hemis * points, levels), absorb, kernel)
    bright = bright.reshape(hemis, points, kernel.shape[1])
    inside = (jnp.arange(points, dtype=jnp.int32) < row_count).astype(F32)
    return bright * inside[None, :, None]


def legendre_rows(legendre, spectral):
    even_odd = jnp.einsum("mpsj,mpsc->mpjc", legendre, spectral, precision=PRECISE)
    return jnp.stack((even_odd[:, 0] + even_odd[:, 1], even_odd[:, 0] - even_odd[:, 1]), axis=1)


def move_coefficients(coefficients, legendre, row_counts, basis, absorb, peak_level, width):
    first = lax.axis_index("spec") * coefficients.shape[2]
    scaled = prior_scale(coefficients, first)
    kernel = channel_kernel(peak_level, width, basis.shape[1])
    spectral = lax.all_to_all(scaled, "spec", split_axis=0, concat_axis=2, tiled=True)
    fourier = legendre_rows(legendre, spectral)
    pieces = lax.all_to_all(fourier, "spec", split_axis=2, concat_axis=0, tiled=True)
    row = synthesize_row(pieces[:, :, 0, :], row_counts[0], basis, absorb, kernel, NLON)
    return row[None]


def split_pair(value):
    high = value.astype(BF16)
    return high, (value - high.astype(F32)).astype(BF16)


def split_constant(value):
    high = lax.reduce_precision(value, exponent_bits=8, mantissa_bits=7)
    return high.astype(BF16), (value - high).astype(BF16)


def arrange_legendre(legendre, first_wave, spec, waves):
    held, _, slots, rows = legendre.shape
    groups, own = held // 4, slots // spec
    lanes = rows * 8

    def body(first_ref, leg_ref, out_ref, turned):
        pair = lax.broadcasted_iota(jnp.int32, (8, slots), 0)
        slot = lax.broadcasted_iota(jnp.int32, (8, slots), 1)
        for group in range(groups):
            degree = first_ref[0] + 4 * group + pair // 2 + 2 * slot + pair % 2
            spread = lax.rsqrt((degree + 1).astype(F32) * waves)
            spread = jnp.where(degree < waves, spread, 0.0)
            block = leg_ref[4 * group:4 * group + 4].reshape(8, rows, slots)
            block = block * spread[:, None, :]
            block = jnp.swapaxes(block, 0, 1).reshape(lanes, slots)
            turned[...] = block.T
            for goal in range(spec):
                out_ref[goal, group * own:(group + 1) * own, :] = turned[goal * own:(goal + 1) * own, :]

    return pl.pallas_call(
        body,
        grid_spec=pltpu.PrefetchScalarGridSpec(
            num_scalar_prefetch=1,
            grid=(1,),
            in_specs=[pl.BlockSpec((held, 2, rows, slots), lambda i, f: (0, 0, 0, 0))],
            out_specs=pl.BlockSpec((spec, groups * own, lanes), lambda i, f: (0, 0, 0)),
            scratch_shapes=[pltpu.VMEM((slots, lanes), F32)],
        ),
        out_shape=jax.ShapeDtypeStruct((spec, groups * own, lanes), F32),
        compiler_params=pltpu.CompilerParams(vmem_limit_bytes=32 << 20),
        cost_estimate=pl.CostEstimate(flops=4_000_000, bytes_accessed=4_000_000, transcendentals=0),
        name="arrange_legendre",
    )(first_wave, jnp.transpose(legendre, (0, 1, 3, 2)))


def partial_rows(order, arranged, padded, sources, own):
    spec, depth, lanes = arranged.shape
    groups = depth // own
    rows = lanes // 8
    half = rows // 2
    columns = padded.shape[-1]

    def body(order_ref, leg_ref, coef_ref, keep_ref, send_ref, spread_ref):
        spread_ref[...] = jnp.zeros_like(spread_ref)
        row = lax.broadcasted_iota(jnp.int32, (lanes, 4 * PAD), 0) % 8
        block = lax.broadcasted_iota(jnp.int32, (lanes, 4 * PAD), 1) // PAD
        here = [row == block, row == block + 4]
        first_core = jnp.full((8, columns), order_ref[3 * sources + half], jnp.int32) == 0
        for group in range(groups):
            piece = leg_ref[0, group * own:(group + 1) * own, :]
            for copy in range(4):
                spread_ref[copy * PAD:copy * PAD + own, :] = piece
            turned = spread_ref[...].T
            parts = [split_pair(jnp.where(mask, turned, 0.0)) for mask in here]
            high = jnp.concatenate([parts[0][0], parts[1][0]], axis=1)
            low = jnp.concatenate([parts[0][1], parts[1][1]], axis=1)
            coef = coef_ref[group]
            total = jnp.dot(high, coef, preferred_element_type=F32) + jnp.dot(low, coef, preferred_element_type=F32)
            for couple in range(half):
                one = total[16 * couple:16 * couple + 8]
                two = total[16 * couple + 8:16 * couple + 16]
                place = order_ref[3 * sources + couple]
                keep_ref[place, 8 * group:8 * group + 8, :] = jnp.where(first_core, one, two)
                send_ref[place, 8 * group:8 * group + 8, :] = jnp.where(first_core, two, one)

    out = jax.ShapeDtypeStruct((half, sources * groups * 8, columns), F32)
    out_spec = pl.BlockSpec((half, groups * 8, columns), lambda i, o: (0, o[2 * sources + i], 0))
    return pl.pallas_call(
        body,
        grid_spec=pltpu.PrefetchScalarGridSpec(
            num_scalar_prefetch=1,
            grid=(sources,),
            in_specs=[
                pl.BlockSpec((1, depth, lanes), lambda i, o: (o[i], 0, 0)),
                pl.BlockSpec((groups, 8 * PAD, columns), lambda i, o: (o[sources + i], 0, 0)),
            ],
            out_specs=[out_spec, out_spec],
            scratch_shapes=[pltpu.VMEM((4 * PAD, lanes), F32)],
        ),
        out_shape=[out, out],
        compiler_params=pltpu.CompilerParams(vmem_limit_bytes=32 << 20),
        cost_estimate=pl.CostEstimate(flops=500_000_000, bytes_accessed=6_000_000, transcendentals=0),
        name="partial_rows",
    )(order, arranged, padded)


def wave_tables(row_count, waves):
    orders = jnp.arange(waves, dtype=jnp.int32)
    weights = jnp.where(orders == 0, 1.0, 2.0) * (2 * orders < row_count).astype(F32)
    coarse = STEP * jnp.arange(NLON // STEP, dtype=jnp.int32)
    places = jnp.concatenate((coarse, jnp.arange(STEP, dtype=jnp.int32)))
    phases = places[:, None] * orders[None, :] % row_count
    angles = 2.0 * math.pi * phases.astype(F32) / row_count.astype(F32)
    gain = jnp.where(jnp.arange(places.shape[0])[:, None] < coarse.shape[0], weights[None, :], 1.0)
    return gain * jnp.cos(angles), gain * jnp.sin(angles)


def synthesize(row_counts, spectra, tables, basis, absorb, kernel):
    waves = spectra.shape[0] // 2
    columns = spectra.shape[1]
    levels = basis.shape[1]
    modes = basis.shape[0]
    channels = kernel.shape[1]
    coarse = NLON // STEP
    tile = 4 * STEP
    zero = jnp.zeros_like(basis)
    widened = jnp.concatenate((basis, zero, zero, -basis), axis=0)
    basis_high, basis_low = split_constant(widened)
    kernel_high, kernel_low = split_constant(kernel)

    def body(count_ref, spec_ref, cos_ref, sin_ref, bh_ref, bl_ref, ab_ref, kh_ref, kl_ref, out_ref, high_ref, low_ref):
        step = pl.program_id(0)

        @pl.when(step == 0)
        def _():
            for parity in range(2):
                value = spec_ref[pl.ds(parity, waves, stride=2), :]
                high, low = split_pair(value)
                high_ref[:, parity * columns:(parity + 1) * columns] = high
                low_ref[:, parity * columns:(parity + 1) * columns] = low

        cos_fine, sin_fine = cos_ref[coarse:, :], sin_ref[coarse:, :]
        cosines, sines = [], []
        for part in range(tile // STEP):
            at = step * (tile // STEP) + part
            cos_at, sin_at = cos_ref[pl.ds(at, 1), :], sin_ref[pl.ds(at, 1), :]
            cosines.append(cos_at * cos_fine - sin_at * sin_fine)
            sines.append(sin_at * cos_fine + cos_at * sin_fine)
        high, low = split_pair(jnp.concatenate(cosines + sines, axis=0))
        fields = jnp.dot(high, high_ref[...], preferred_element_type=F32)
        fields += jnp.dot(low, high_ref[...], preferred_element_type=F32)
        fields += jnp.dot(high, low_ref[...], preferred_element_type=F32)
        even, odd = fields[:, :columns], fields[:, columns:]
        north, south = even + odd, even - odd
        both = jnp.concatenate(
            [jnp.concatenate([side[:tile], side[tile:]], axis=1) for side in (north, south)], axis=0
        )
        high, low = split_pair(both)
        temps = jnp.dot(high, bh_ref[...], preferred_element_type=F32)
        temps += jnp.dot(low, bh_ref[...], preferred_element_type=F32)
        temps += jnp.dot(high, bl_ref[...], preferred_element_type=F32)
        source = jnp.exp(0.5 * temps)
        layers = ab_ref[...] * source
        above = lax.broadcasted_iota(jnp.int32, (2 * levels, levels), 0) % levels
        level = lax.broadcasted_iota(jnp.int32, (2 * levels, levels), 1)
        upper = jnp.where(above < level, 1.0, 0.0).astype(BF16)
        overhead = jnp.dot(jnp.concatenate(split_pair(layers), axis=1), upper, preferred_element_type=F32)
        half = jnp.tanh(0.5 * layers)
        emitted = source * jnp.exp(-overhead) * (2.0 * half / (1.0 + half))
        high, low = split_pair(emitted)
        bright = jnp.dot(high, kh_ref[...], preferred_element_type=F32)
        bright += jnp.dot(low, kh_ref[...], preferred_element_type=F32)
        bright += jnp.dot(high, kl_ref[...], preferred_element_type=F32)
        place = step * tile + lax.broadcasted_iota(jnp.int32, (2 * tile, 1), 0) % tile
        bright = jnp.where(place < count_ref[0], bright, 0.0)
        out_ref[0] = bright.reshape(2, tile, channels)

    def whole(array):
        return pl.BlockSpec(array.shape, lambda i, c: (0,) * array.ndim)

    operands = (spectra, *tables, basis_high, basis_low, absorb[None, :], kernel_high, kernel_low)
    return pl.pallas_call(
        body,
        grid_spec=pltpu.PrefetchScalarGridSpec(
            num_scalar_prefetch=1,
            grid=(NLON // tile,),
            in_specs=[whole(array) for array in operands],
            out_specs=pl.BlockSpec((1, 2, tile, channels), lambda i, c: (0, 0, i, 0)),
            scratch_shapes=[pltpu.VMEM((waves, 2 * columns), BF16)] * 2,
        ),
        out_shape=jax.ShapeDtypeStruct((1, 2, NLON, channels), F32),
        compiler_params=pltpu.CompilerParams(vmem_limit_bytes=48 << 20),
        cost_estimate=pl.CostEstimate(flops=4_000_000_000, bytes_accessed=8_000_000, transcendentals=2_000_000),
        name="synthesize",
    )(row_counts, *operands)


def move_legendre(spec, coefficients, legendre, row_counts, basis, absorb, peak_level, width):
    waves, _, own, columns = coefficients.shape
    held = legendre.shape[0]
    groups = held // 4
    me = lax.axis_index("spec").astype(jnp.int32)
    arranged = arrange_legendre(legendre, (me * held)[None], spec, waves)
    arrived = lax.all_to_all(arranged, "spec", split_axis=0, concat_axis=0, tiled=True)
    padded = jnp.pad(coefficients, ((0, 0), (0, 0), (0, PAD - own), (0, 0)))
    padded = padded.reshape(waves // 4, 8 * PAD, columns)
    tables = wave_tables(row_counts[0], waves)
    kernel = channel_kernel(peak_level, width, basis.shape[1])

    def swap(value, distance):
        return lax.ppermute(value, "spec", [(i, i ^ distance) for i in range(spec)])

    sources = spec // PLANES
    couple = jnp.arange(spec // 2, dtype=jnp.int32) ^ (me >> 1)
    place = (couple & 1) * (spec // 4) + (couple >> 1)
    pieces = []
    for plane in range(PLANES):
        local = jnp.arange(sources, dtype=jnp.int32)
        source = plane * sources + local
        order = jnp.concatenate((source, source, local, place, (me & 1)[None]))
        keep, send = partial_rows(order, arrived, padded, sources, own)
        other = swap(send, 1)
        quarter = spec // 4
        send, keep = keep[quarter:] + other[quarter:], keep[:quarter] + other[:quarter]
        both = keep + swap(send, 2)
        total = both[0]
        for away in range(1, quarter):
            total = total + swap(both[away], 4 * away)
        pieces.append(total)
    spectra = jnp.concatenate(pieces, axis=0)
    return synthesize(row_counts, spectra, tables, basis, absorb, kernel)


def solution(mesh):
    spec = mesh.shape["spec"]
    placed = (
        P("draws", None, "spec", None),
        P("spec", None, None, None),
        P("spec"),
        P(),
        P(),
        P(),
        P(),
    )

    def on_device(coefficients, legendre, *others):
        held, _, _, rows = legendre.shape
        own = coefficients.shape[2]
        small = rows == spec and 8 * rows == 4 * PAD and held % 4 == 0 and rows <= own <= PAD
        if small:
            return move_legendre(spec, coefficients, legendre, *others)
        return move_coefficients(coefficients, legendre, *others)

    return jax.shard_map(
        on_device,
        mesh=mesh,
        in_specs=placed,
        out_specs=P(("draws", "spec"), None, None, None),
        check_vma=False,
    )
```

```python
import functools
import math

import jax
import jax.numpy as jnp
from jax import lax
from jax.experimental import pallas as pl
from jax.experimental.pallas import tpu as pltpu
from jax.sharding import PartitionSpec as P

NLON = 1280
STEP = 32
PLANES = 4
LANES = 128

PRECISE = lax.Precision.HIGHEST
F32 = jnp.float32
BF16 = jnp.bfloat16


def prior_scale(shard, first):
    waves = shard.shape[0]
    slots = shard.shape[2]
    orders = jnp.arange(waves, dtype=jnp.int32)[:, None, None]
    parity = jnp.arange(2, dtype=jnp.int32)[None, :, None]
    slot_index = first + jnp.arange(slots, dtype=jnp.int32)[None, None, :]
    degree = orders + 2 * slot_index + parity
    spread = lax.rsqrt((degree + 1).astype(F32) * waves)
    spread = jnp.where(degree < waves, spread, jnp.zeros_like(spread))
    return shard.astype(F32) * spread[..., None]


def channel_kernel(peak_level, width, levels):
    height = jnp.arange(levels, dtype=F32)[:, None]
    offsets = (height - peak_level.astype(F32)[None, :]) / width[None, :]
    weights = jnp.exp(-offsets * offsets)
    return weights / jnp.sum(weights, axis=0, keepdims=True)


def radiate(temps, absorb, kernel):
    levels = temps.shape[-1]
    strict_upper = (jnp.arange(levels)[:, None] < jnp.arange(levels)[None, :]).astype(F32)
    source = jnp.exp(0.5 * temps)
    layers = absorb[None, :] * source
    overhead = jnp.dot(layers, strict_upper, precision=PRECISE, preferred_element_type=F32)
    emitted = source * jnp.exp(-overhead) * -jnp.expm1(-layers)
    return jnp.dot(emitted, kernel, precision=PRECISE, preferred_element_type=F32)


def fourier_lookup(row_count, waves, points):
    orders = jnp.arange(waves, dtype=jnp.int32)
    places = jnp.arange(points, dtype=jnp.int32)
    phases = places[:, None] * orders[None, :] % row_count
    angles = 2.0 * math.pi * phases.astype(F32) / row_count.astype(F32)
    weights = jnp.where(orders == 0, 1.0, 2.0) * (2 * orders < row_count).astype(F32)
    return jnp.stack((weights * jnp.cos(angles), -weights * jnp.sin(angles)), axis=-1)


def synthesize_row(spectra, row_count, modes_basis, absorb, kernel, points):
    waves, hemis, columns = spectra.shape
    lookup = fourier_lookup(row_count, waves, points)
    split_parts = spectra.reshape(waves, hemis, 2, columns // 2)
    fields = jnp.einsum("kmq,mhqc->hkc", lookup, split_parts, precision=PRECISE)
    fields = jnp.einsum("hkc,cl->hkl", fields, modes_basis, precision=PRECISE)
    levels = fields.shape[-1]
    bright = radiate(fields.reshape(hemis * points, levels), absorb, kernel)
    bright = bright.reshape(hemis, points, kernel.shape[1])
    inside = (jnp.arange(points, dtype=jnp.int32) < row_count).astype(F32)
    return bright * inside[None, :, None]


def legendre_rows(legendre, spectral):
    even_odd = jnp.einsum("mpsj,mpsc->mpjc", legendre, spectral, precision=PRECISE)
    return jnp.stack((even_odd[:, 0] + even_odd[:, 1], even_odd[:, 0] - even_odd[:, 1]), axis=1)


def move_coefficients(coefficients, legendre, row_counts, basis, absorb, peak_level, width):
    first = lax.axis_index("spec") * coefficients.shape[2]
    scaled = prior_scale(coefficients, first)
    kernel = channel_kernel(peak_level, width, basis.shape[1])
    spectral = lax.all_to_all(scaled, "spec", split_axis=0, concat_axis=2, tiled=True)
    fourier = legendre_rows(legendre, spectral)
    pieces = lax.all_to_all(fourier, "spec", split_axis=2, concat_axis=0, tiled=True)
    row = synthesize_row(pieces[:, :, 0, :], row_counts[0], basis, absorb, kernel, NLON)
    return row[None]


def split_pair(value):
    high = value.astype(BF16)
    return high, (value - high.astype(F32)).astype(BF16)


def split_constant(value):
    high = lax.reduce_precision(value, exponent_bits=8, mantissa_bits=7)
    return high.astype(BF16), (value - high).astype(BF16)


def arrange_legendre(legendre, me, spec, waves):
    held, _, slots, rows = legendre.shape
    groups, own = held // 4, slots // spec
    lanes = rows * 8

    def body(me_ref, leg_ref, out_ref, turned):
        pair = lax.broadcasted_iota(jnp.int32, (8, slots), 0)
        slot = lax.broadcasted_iota(jnp.int32, (8, slots), 1)
        for group in range(groups):
            degree = me_ref[0] * held + 4 * group + pair // 2 + 2 * slot + pair % 2
            spread = lax.rsqrt((degree + 1).astype(F32) * waves)
            spread = jnp.where(degree < waves, spread, 0.0)
            block = leg_ref[4 * group:4 * group + 4].reshape(8, rows, slots)
            block = block * spread[:, None, :]
            block = jnp.swapaxes(block, 0, 1).reshape(lanes, slots)
            turned[...] = block.T
            for goal in range(spec):
                piece = turned[goal * own:(goal + 1) * own, :]
                out_ref[goal, group * own:(group + 1) * own, :] = piece

    return pl.pallas_call(
        body,
        grid_spec=pltpu.PrefetchScalarGridSpec(
            num_scalar_prefetch=1,
            grid=(1,),
            in_specs=[pl.BlockSpec((held, 2, rows, slots), lambda i, f: (0, 0, 0, 0))],
            out_specs=pl.BlockSpec((spec, groups * own, lanes), lambda i, f: (0, 0, 0)),
            scratch_shapes=[pltpu.VMEM((slots, lanes), F32)],
        ),
        out_shape=jax.ShapeDtypeStruct((spec, groups * own, lanes), F32),
        compiler_params=pltpu.CompilerParams(vmem_limit_bytes=32 << 20),
        cost_estimate=pl.CostEstimate(flops=1, bytes_accessed=1, transcendentals=0),
        name="arrange_legendre",
    )(me[None], jnp.transpose(legendre, (0, 1, 3, 2)))


def partial_rows(order, arranged, coefficients, plane, own):
    spec, depth, lanes = arranged.shape
    sources = spec // PLANES
    groups = depth // own
    half = lanes // 16
    columns = coefficients.shape[-1]
    span = 8 * own

    def body(order_ref, leg_ref, coef_ref, keep_ref, send_ref, spread_ref):
        row = lax.broadcasted_iota(jnp.int32, (lanes, span), 0) % 8
        inner = lax.broadcasted_iota(jnp.int32, (lanes, span), 1)
        here = row == 2 * (inner // (2 * own)) + inner % 2
        first_core = jnp.full((8, columns), order_ref[half], jnp.int32) == 0
        for group in range(groups):
            piece = leg_ref[0, group * own:(group + 1) * own, :]
            for copy in range(4):
                for parity in range(2):
                    spread_ref[pl.ds(2 * own * copy + parity, own, stride=2), :] = piece
            high, low = split_pair(jnp.where(here, spread_ref[...].T, 0.0))
            coef = coef_ref[span * group:span * (group + 1), :]
            total = jnp.dot(high, coef, preferred_element_type=F32) + jnp.dot(low, coef, preferred_element_type=F32)
            for couple in range(half):
                one = total[16 * couple:16 * couple + 8]
                two = total[16 * couple + 8:16 * couple + 16]
                place = order_ref[couple]
                keep_ref[place, 8 * group:8 * group + 8, :] = jnp.where(first_core, one, two)
                send_ref[place, 8 * group:8 * group + 8, :] = jnp.where(first_core, two, one)

    out = jax.ShapeDtypeStruct((half, sources * groups * 8, columns), F32)
    out_spec = pl.BlockSpec((half, groups * 8, columns), lambda i, o: (0, i, 0))
    return pl.pallas_call(
        body,
        grid_spec=pltpu.PrefetchScalarGridSpec(
            num_scalar_prefetch=1,
            grid=(sources,),
            in_specs=[
                pl.BlockSpec((1, depth, lanes), lambda i, o: (plane * sources + i, 0, 0)),
                pl.BlockSpec((groups * span, columns), lambda i, o: (plane * sources + i, 0)),
            ],
            out_specs=[out_spec, out_spec],
            scratch_shapes=[pltpu.VMEM((span, lanes), F32)],
        ),
        out_shape=[out, out],
        compiler_params=pltpu.CompilerParams(vmem_limit_bytes=32 << 20),
        cost_estimate=pl.CostEstimate(flops=1, bytes_accessed=1, transcendentals=0),
        name="partial_rows",
    )(order, arranged, coefficients)


def wave_tables(row_count, waves):
    orders = jnp.arange(waves, dtype=jnp.int32)
    weights = jnp.where(orders == 0, 1.0, 2.0) * (2 * orders < row_count).astype(F32)
    steps = NLON // STEP
    coarse = STEP * jnp.arange(steps, dtype=jnp.int32)
    places = jnp.concatenate((coarse, jnp.arange(STEP, dtype=jnp.int32)))
    phases = places[:, None] * orders[None, :] % row_count
    angles = 2.0 * math.pi * phases.astype(F32) / row_count.astype(F32)
    gain = jnp.where(jnp.arange(places.shape[0])[:, None] < steps, weights[None, :], 1.0)
    bases = (gain * jnp.cos(angles), gain * jnp.sin(angles))
    parts = 8

    def body(cos_ref, sin_ref, ch_ref, cl_ref, sh_ref, sl_ref):
        cos_fine, sin_fine = cos_ref[steps:, :], sin_ref[steps:, :]
        for part in range(parts):
            at = pl.program_id(0) * parts + part
            cos_at, sin_at = cos_ref[pl.ds(at, 1), :], sin_ref[pl.ds(at, 1), :]
            here = slice(part * STEP, (part + 1) * STEP)
            ch_ref[here, :], cl_ref[here, :] = split_pair(cos_at * cos_fine - sin_at * sin_fine)
            sh_ref[here, :], sl_ref[here, :] = split_pair(sin_at * cos_fine + cos_at * sin_fine)

    tile = parts * STEP
    return pl.pallas_call(
        body,
        grid=(NLON // tile,),
        in_specs=[pl.BlockSpec(bases[0].shape, lambda i: (0, 0))] * 2,
        out_specs=[pl.BlockSpec((tile, waves), lambda i: (i, 0))] * 4,
        out_shape=[jax.ShapeDtypeStruct((NLON, waves), BF16)] * 4,
        compiler_params=pltpu.CompilerParams(vmem_limit_bytes=32 << 20),
        cost_estimate=pl.CostEstimate(flops=1, bytes_accessed=1, transcendentals=0),
        name="wave_tables",
    )(*bases)


def synthesize(scalars, spectra, tables, basis, absorb, kernel):
    planes, deep, columns = spectra.shape
    span = deep // 2
    waves = planes * span
    levels = basis.shape[1]
    channels = kernel.shape[1]
    tile = 8 * STEP
    zero = jnp.zeros_like(basis)
    widened = jnp.concatenate((basis, zero, zero, -basis), axis=0)
    basis_high, basis_low = split_constant(widened)
    kernel_high, kernel_low = split_constant(kernel)

    def body(scalar_ref, spec_ref, ch_ref, cl_ref, sh_ref, sl_ref, bh_ref, bl_ref, ab_ref, kh_ref, kl_ref,
             out_ref, high_ref, low_ref):
        step = pl.program_id(0)

        @pl.when(step == 0)
        def _():
            for plane in range(planes):
                here = pl.ds(pl.multiple_of(scalar_ref[1 + plane] * span, 16), span)
                for parity in range(2):
                    high, low = split_pair(spec_ref[plane, pl.ds(parity, span, stride=2), :])
                    high_ref[here, parity * columns:(parity + 1) * columns] = high
                    low_ref[here, parity * columns:(parity + 1) * columns] = low

        sides = []
        for first_ref, second_ref in ((ch_ref, cl_ref), (sh_ref, sl_ref)):
            fields = jnp.dot(first_ref[...], high_ref[...], preferred_element_type=F32)
            fields += jnp.dot(second_ref[...], high_ref[...], preferred_element_type=F32)
            fields += jnp.dot(first_ref[...], low_ref[...], preferred_element_type=F32)
            even, odd = fields[:, :columns], fields[:, columns:]
            sides.append((even + odd, even - odd))
        both = jnp.concatenate(
            [jnp.concatenate([sides[0][side], sides[1][side]], axis=1) for side in range(2)], axis=0
        )
        high, low = split_pair(both)
        temps = jnp.dot(high, bh_ref[...], preferred_element_type=F32)
        temps += jnp.dot(low, bh_ref[...], preferred_element_type=F32)
        temps += jnp.dot(high, bl_ref[...], preferred_element_type=F32)
        source = jnp.exp(0.5 * temps)
        layers = ab_ref[...] * source
        above = lax.broadcasted_iota(jnp.int32, (2 * levels, levels), 0) % levels
        level = lax.broadcasted_iota(jnp.int32, (2 * levels, levels), 1)
        upper = jnp.where(above < level, 1.0, 0.0).astype(BF16)
        overhead = jnp.dot(jnp.concatenate(split_pair(layers), axis=1), upper, preferred_element_type=F32)
        half = jnp.tanh(0.5 * layers)
        emitted = source * jnp.exp(-overhead) * (2.0 * half / (1.0 + half))
        high, low = split_pair(emitted)
        bright = jnp.dot(high, kh_ref[...], preferred_element_type=F32)
        bright += jnp.dot(low, kh_ref[...], preferred_element_type=F32)
        bright += jnp.dot(high, kl_ref[...], preferred_element_type=F32)
        place = step * tile + lax.broadcasted_iota(jnp.int32, (2 * tile, 1), 0) % tile
        bright = jnp.where(place < scalar_ref[0], bright, 0.0)
        out_ref[0] = bright.reshape(2, tile, channels)

    def whole(array):
        return pl.BlockSpec(array.shape, lambda i, c: (0,) * array.ndim)

    constants = (basis_high, basis_low, absorb[None, :], kernel_high, kernel_low)
    table_spec = pl.BlockSpec((tile, waves), lambda i, c: (i, 0))
    return pl.pallas_call(
        body,
        grid_spec=pltpu.PrefetchScalarGridSpec(
            num_scalar_prefetch=1,
            grid=(NLON // tile,),
            in_specs=[whole(spectra)] + [table_spec] * 4 + [whole(array) for array in constants],
            out_specs=pl.BlockSpec((1, 2, tile, channels), lambda i, c: (0, 0, i, 0)),
            scratch_shapes=[pltpu.VMEM((waves, 2 * columns), BF16)] * 2,
        ),
        out_shape=jax.ShapeDtypeStruct((1, 2, NLON, channels), F32),
        compiler_params=pltpu.CompilerParams(vmem_limit_bytes=48 << 20),
        cost_estimate=pl.CostEstimate(flops=1, bytes_accessed=1, transcendentals=0),
        name="synthesize",
    )(scalars, spectra, *tables, *constants)


def move_legendre(spec, coefficients, legendre, row_counts, basis, absorb, peak_level, width):
    waves, _, own, columns = coefficients.shape
    held = legendre.shape[0]
    sources = spec // PLANES
    quarter = spec // 4
    me = lax.axis_index("spec").astype(jnp.int32)
    natural = jnp.transpose(coefficients, (0, 2, 1, 3)).reshape(waves * 2 * own, columns)

    def swap(value, distance, use=None):
        pairs = [(i, i ^ distance) for i in range(spec) if use is None or use(i)]
        return lax.ppermute(value, "spec", pairs)

    def after(values, earlier):
        return lax.optimization_barrier((values, earlier))[0]

    arranged = arrange_legendre(legendre, me, spec, waves)
    tables = wave_tables(row_counts[0], waves)
    kernel = channel_kernel(peak_level, width, basis.shape[1])
    arrived = lax.all_to_all(arranged, "spec", split_axis=0, concat_axis=0, tiled=True)
    arrived = after(arrived, (tables, kernel))
    couple = jnp.arange(spec // 2, dtype=jnp.int32) ^ (me >> 1)
    order = jnp.concatenate(((couple & 1) * quarter + (couple >> 1), (me & 1)[None]))

    def contract(plane, earlier=()):
        return partial_rows(after(order, earlier), arrived, natural, plane, own)

    def add_cores(keep, other):
        return keep[quarter:] + other[quarter:], keep[:quarter] + other[:quarter]

    def between_planes(value, plane):
        use = lambda i: (plane * held + 2 * (i // sources) * own) * sources < waves
        return [swap(value[away], sources * away, use) for away in range(1, PLANES)]

    keep3, send3 = contract(3)
    keep0, send0 = contract(0, send3)
    keep1, send1 = contract(1, send0)
    both3 = keep3 + swap(send3, 1)
    early = between_planes(jnp.swapaxes(both3.reshape(2, quarter, *both3.shape[1:]), 0, 1), 3)
    side0, own0 = add_cores(keep0, swap(send0, 1))
    keep2, send2 = contract(2, (side0, both3, send1))
    sum0 = own0 + swap(side0, 2)
    side1, own1 = add_cores(keep1, swap(send1, 1))
    late0 = between_planes(sum0, 0)

    keep2, other2 = after((keep2, swap(send2, 1)), (sum0, side1))
    side2, own2 = add_cores(keep2, other2)
    sum1 = own1 + swap(side1, 2)
    late1 = between_planes(sum1, 1)
    sum3 = both3.reshape(2, quarter, *both3.shape[1:])[:, 0] + sum(early)
    sum3 = sum3[0] + swap(after(sum3[1], side2), 2)
    sum2 = own2 + swap(side2, 2)
    late2 = between_planes(after(sum2, late0), 2)
    spectra = jnp.stack([sum0[0] + sum(late0), sum1[0] + sum(late1), sum2[0] + sum(late2), sum3])
    scalars = jnp.concatenate((row_counts, jnp.arange(PLANES, dtype=jnp.int32)))
    return synthesize(scalars, spectra, tables, basis, absorb, kernel)


def solution(mesh):
    spec = mesh.shape["spec"]
    placed = (
        P("draws", None, "spec", None),
        P("spec", None, None, None),
        P("spec"),
        P(),
        P(),
        P(),
        P(),
    )

    def on_device(coefficients, legendre, *others):
        held, _, _, rows = legendre.shape
        own = coefficients.shape[2]
        if rows == spec and 8 * rows == LANES and held % 8 == 0 and rows <= own:
            return move_legendre(spec, coefficients, legendre, *others)
        return move_coefficients(coefficients, legendre, *others)

    return jax.shard_map(
        on_device,
        mesh=mesh,
        in_specs=placed,
        out_specs=P(("draws", "spec"), None, None, None),
        check_vma=False,
    )
```

```python
import functools
import math

import jax
import jax.numpy as jnp
from jax import lax
from jax.experimental import pallas as pl
from jax.experimental.pallas import tpu as pltpu
from jax.sharding import PartitionSpec as P

NLON = 1280
STEP = 32
PLANES = 4
HALVES = 1
LANES = 128

PRECISE = lax.Precision.HIGHEST
F32 = jnp.float32
BF16 = jnp.bfloat16


def prior_scale(shard, first):
    waves = shard.shape[0]
    slots = shard.shape[2]
    orders = jnp.arange(waves, dtype=jnp.int32)[:, None, None]
    parity = jnp.arange(2, dtype=jnp.int32)[None, :, None]
    slot_index = first + jnp.arange(slots, dtype=jnp.int32)[None, None, :]
    degree = orders + 2 * slot_index + parity
    spread = lax.rsqrt((degree + 1).astype(F32) * waves)
    spread = jnp.where(degree < waves, spread, jnp.zeros_like(spread))
    return shard.astype(F32) * spread[..., None]


def channel_kernel(peak_level, width, levels):
    height = jnp.arange(levels, dtype=F32)[:, None]
    offsets = (height - peak_level.astype(F32)[None, :]) / width[None, :]
    weights = jnp.exp(-offsets * offsets)
    return weights / jnp.sum(weights, axis=0, keepdims=True)


def radiate(temps, absorb, kernel):
    levels = temps.shape[-1]
    strict_upper = (jnp.arange(levels)[:, None] < jnp.arange(levels)[None, :]).astype(F32)
    source = jnp.exp(0.5 * temps)
    layers = absorb[None, :] * source
    overhead = jnp.dot(layers, strict_upper, precision=PRECISE, preferred_element_type=F32)
    emitted = source * jnp.exp(-overhead) * -jnp.expm1(-layers)
    return jnp.dot(emitted, kernel, precision=PRECISE, preferred_element_type=F32)


def fourier_lookup(row_count, waves, points):
    orders = jnp.arange(waves, dtype=jnp.int32)
    places = jnp.arange(points, dtype=jnp.int32)
    phases = places[:, None] * orders[None, :] % row_count
    angles = 2.0 * math.pi * phases.astype(F32) / row_count.astype(F32)
    weights = jnp.where(orders == 0, 1.0, 2.0) * (2 * orders < row_count).astype(F32)
    return jnp.stack((weights * jnp.cos(angles), -weights * jnp.sin(angles)), axis=-1)


def synthesize_row(spectra, row_count, modes_basis, absorb, kernel, points):
    waves, hemis, columns = spectra.shape
    lookup = fourier_lookup(row_count, waves, points)
    split_parts = spectra.reshape(waves, hemis, 2, columns // 2)
    fields = jnp.einsum("kmq,mhqc->hkc", lookup, split_parts, precision=PRECISE)
    fields = jnp.einsum("hkc,cl->hkl", fields, modes_basis, precision=PRECISE)
    levels = fields.shape[-1]
    bright = radiate(fields.reshape(hemis * points, levels), absorb, kernel)
    bright = bright.reshape(hemis, points, kernel.shape[1])
    inside = (jnp.arange(points, dtype=jnp.int32) < row_count).astype(F32)
    return bright * inside[None, :, None]


def legendre_rows(legendre, spectral):
    even_odd = jnp.einsum("mpsj,mpsc->mpjc", legendre, spectral, precision=PRECISE)
    return jnp.stack((even_odd[:, 0] + even_odd[:, 1], even_odd[:, 0] - even_odd[:, 1]), axis=1)


def move_coefficients(coefficients, legendre, row_counts, basis, absorb, peak_level, width):
    first = lax.axis_index("spec") * coefficients.shape[2]
    scaled = prior_scale(coefficients, first)
    kernel = channel_kernel(peak_level, width, basis.shape[1])
    spectral = lax.all_to_all(scaled, "spec", split_axis=0, concat_axis=2, tiled=True)
    fourier = legendre_rows(legendre, spectral)
    pieces = lax.all_to_all(fourier, "spec", split_axis=2, concat_axis=0, tiled=True)
    row = synthesize_row(pieces[:, :, 0, :], row_counts[0], basis, absorb, kernel, NLON)
    return row[None]


def split_pair(value):
    high = value.astype(BF16)
    return high, (value - high.astype(F32)).astype(BF16)


def split_constant(value):
    high = lax.reduce_precision(value, exponent_bits=8, mantissa_bits=7)
    return high.astype(BF16), (value - high).astype(BF16)


def arrange_legendre(legendre, me, spec, waves):
    held, _, slots, rows = legendre.shape
    groups, own = held // 4, slots // spec
    lanes = rows * 8
    share = groups // HALVES

    def body(me_ref, leg_ref, *refs):
        turned = refs[-1]
        pair = lax.broadcasted_iota(jnp.int32, (8, slots), 0)
        slot = lax.broadcasted_iota(jnp.int32, (8, slots), 1)
        for group in range(groups):
            degree = me_ref[0] * held + 4 * group + pair // 2 + 2 * slot + pair % 2
            spread = lax.rsqrt((degree + 1).astype(F32) * waves)
            spread = jnp.where(degree < waves, spread, 0.0)
            block = leg_ref[4 * group:4 * group + 4].reshape(8, rows, slots)
            block = block * spread[:, None, :]
            block = jnp.swapaxes(block, 0, 1).reshape(lanes, slots)
            turned[...] = block.T
            for goal in range(spec):
                piece = turned[goal * own:(goal + 1) * own, :]
                at = group % share
                refs[group // share][goal, at * own:(at + 1) * own, :] = piece

    return pl.pallas_call(
        body,
        grid_spec=pltpu.PrefetchScalarGridSpec(
            num_scalar_prefetch=1,
            grid=(1,),
            in_specs=[pl.BlockSpec((held, 2, rows, slots), lambda i, f: (0, 0, 0, 0))],
            out_specs=[pl.BlockSpec((spec, share * own, lanes), lambda i, f: (0, 0, 0))] * HALVES,
            scratch_shapes=[pltpu.VMEM((slots, lanes), F32)],
        ),
        out_shape=[jax.ShapeDtypeStruct((spec, share * own, lanes), F32)] * HALVES,
        compiler_params=pltpu.CompilerParams(vmem_limit_bytes=32 << 20),
        cost_estimate=pl.CostEstimate(flops=1, bytes_accessed=1, transcendentals=0),
        name="arrange_legendre",
    )(me[None], jnp.transpose(legendre, (0, 1, 3, 2)))


def partial_rows(order, arranged, coefficients, first, sources, half_at, own):
    _, depth, lanes = arranged.shape
    groups = depth // own
    half = lanes // 16
    columns = coefficients.shape[-1]
    span = 8 * own

    def body(order_ref, leg_ref, coef_ref, keep_ref, send_ref, spread_ref):
        row = lax.broadcasted_iota(jnp.int32, (lanes, span), 0) % 8
        inner = lax.broadcasted_iota(jnp.int32, (lanes, span), 1)
        here = row == 2 * (inner // (2 * own)) + inner % 2
        first_core = jnp.full((8, columns), order_ref[half], jnp.int32) == 0
        for group in range(groups):
            piece = leg_ref[0, group * own:(group + 1) * own, :]
            for copy in range(4):
                for parity in range(2):
                    spread_ref[pl.ds(2 * own * copy + parity, own, stride=2), :] = piece
            high, low = split_pair(jnp.where(here, spread_ref[...].T, 0.0))
            coef = coef_ref[span * group:span * (group + 1), :]
            total = jnp.dot(high, coef, preferred_element_type=F32) + jnp.dot(low, coef, preferred_element_type=F32)
            for couple in range(half):
                one = total[16 * couple:16 * couple + 8]
                two = total[16 * couple + 8:16 * couple + 16]
                place = order_ref[couple]
                keep_ref[place, 8 * group:8 * group + 8, :] = jnp.where(first_core, one, two)
                send_ref[place, 8 * group:8 * group + 8, :] = jnp.where(first_core, two, one)

    out = jax.ShapeDtypeStruct((half, sources * groups * 8, columns), F32)
    out_spec = pl.BlockSpec((half, groups * 8, columns), lambda i, o: (0, i, 0))
    return pl.pallas_call(
        body,
        grid_spec=pltpu.PrefetchScalarGridSpec(
            num_scalar_prefetch=1,
            grid=(sources,),
            in_specs=[
                pl.BlockSpec((1, depth, lanes), lambda i, o: (first + i, 0, 0)),
                pl.BlockSpec((groups * span, columns), lambda i, o: (HALVES * (first + i) + half_at, 0)),
            ],
            out_specs=[out_spec, out_spec],
            scratch_shapes=[pltpu.VMEM((span, lanes), F32)],
        ),
        out_shape=[out, out],
        compiler_params=pltpu.CompilerParams(vmem_limit_bytes=32 << 20),
        cost_estimate=pl.CostEstimate(flops=1, bytes_accessed=1, transcendentals=0),
        name="partial_rows",
    )(order, arranged, coefficients)


def wave_tables(row_count, orders):
    steps = NLON // STEP
    coarse = STEP * jnp.arange(steps, dtype=jnp.int32)
    places = jnp.concatenate((coarse, jnp.arange(STEP, dtype=jnp.int32)))[:, None]
    bases = []
    for order in orders:
        weights = jnp.where(order == 0, 1.0, 2.0) * (2 * order < row_count).astype(F32)
        angles = 2.0 * math.pi * (places * order[None, :] % row_count).astype(F32) / row_count.astype(F32)
        gain = jnp.where(jnp.arange(places.shape[0])[:, None] < steps, weights[None, :], 1.0)
        bases += [gain * jnp.cos(angles), gain * jnp.sin(angles)]
    parts = 8

    def body(*refs):
        for at in range(0, len(bases), 2):
            cos_ref, sin_ref = refs[at], refs[at + 1]
            cos_fine, sin_fine = cos_ref[steps:, :], sin_ref[steps:, :]
            for part in range(parts):
                step = pl.program_id(0) * parts + part
                here = slice(part * STEP, (part + 1) * STEP)
                cos_at, sin_at = cos_ref[pl.ds(step, 1), :], sin_ref[pl.ds(step, 1), :]
                both = (cos_at * cos_fine - sin_at * sin_fine, sin_at * cos_fine + cos_at * sin_fine)
                for kind in range(2):
                    high, low = split_pair(both[kind])
                    refs[len(bases) + at + kind][here, :] = jnp.concatenate([high, low, high], axis=1)

    tile = parts * STEP
    return pl.pallas_call(
        body,
        grid=(NLON // tile,),
        in_specs=[pl.BlockSpec(base.shape, lambda i: (0, 0)) for base in bases],
        out_specs=[pl.BlockSpec((tile, 3 * base.shape[1]), lambda i: (i, 0)) for base in bases],
        out_shape=[jax.ShapeDtypeStruct((NLON, 3 * base.shape[1]), BF16) for base in bases],
        compiler_params=pltpu.CompilerParams(vmem_limit_bytes=32 << 20),
        cost_estimate=pl.CostEstimate(flops=1, bytes_accessed=1, transcendentals=0),
        name="wave_tables",
    )(*bases)


def stack_spectra(spec_ref, stack_ref):
    waves, columns = spec_ref.shape[0] // 2, spec_ref.shape[1]
    for parity in range(2):
        high, low = split_pair(spec_ref[pl.ds(parity, waves, stride=2), :])
        here = slice(parity * columns, (parity + 1) * columns)
        stack_ref[:waves, here] = high
        stack_ref[waves:2 * waves, here] = high
        stack_ref[2 * waves:, here] = low


def fourier_sums(spectra, tables):
    deep, columns = spectra.shape
    depth = deep // 2 * 3
    tile = 8 * STEP

    def body(spec_ref, cos_ref, sin_ref, out_ref, stack_ref):
        @pl.when(pl.program_id(0) == 0)
        def _():
            stack_spectra(spec_ref, stack_ref)

        for kind, table_ref in enumerate((cos_ref, sin_ref)):
            here = slice(2 * kind * columns, 2 * (kind + 1) * columns)
            out_ref[:, here] = jnp.dot(table_ref[...], stack_ref[...], preferred_element_type=F32)

    return pl.pallas_call(
        body,
        grid=(NLON // tile,),
        in_specs=[pl.BlockSpec((deep, columns), lambda i: (0, 0))]
        + [pl.BlockSpec((tile, depth), lambda i: (i, 0))] * 2,
        out_specs=pl.BlockSpec((tile, 4 * columns), lambda i: (i, 0)),
        out_shape=jax.ShapeDtypeStruct((NLON, 4 * columns), F32),
        scratch_shapes=[pltpu.VMEM((depth, 2 * columns), BF16)],
        compiler_params=pltpu.CompilerParams(vmem_limit_bytes=32 << 20),
        cost_estimate=pl.CostEstimate(flops=1, bytes_accessed=1, transcendentals=0),
        name="fourier_sums",
    )(spectra, *tables)


def synthesize(row_counts, first_sums, spectra, tables, basis, absorb, kernel_high, kernel_low):
    deep, columns = spectra.shape
    depth = deep // 2 * 3
    levels = basis.shape[1]
    channels = kernel_high.shape[1]
    tile = 8 * STEP
    zero = jnp.zeros_like(basis)
    widened = jnp.concatenate((basis, zero, zero, -basis), axis=0)
    basis_high, basis_low = split_constant(widened)
    kernel_twice = jnp.concatenate((kernel_high, kernel_high), axis=0)

    def body(count_ref, sums_ref, spec_ref, cos_ref, sin_ref, bh_ref, bl_ref, ab_ref, kh_ref, kl_ref, out_ref, stack_ref):
        step = pl.program_id(0)

        @pl.when(step == 0)
        def _():
            stack_spectra(spec_ref, stack_ref)

        sides = []
        for kind, table_ref in enumerate((cos_ref, sin_ref)):
            fields = jnp.dot(table_ref[...], stack_ref[...], preferred_element_type=F32)
            fields += sums_ref[:, 2 * kind * columns:2 * (kind + 1) * columns]
            even, odd = fields[:, :columns], fields[:, columns:]
            sides.append((even + odd, even - odd))
        for side in range(2):
            high, low = split_pair(jnp.concatenate([sides[0][side], sides[1][side]], axis=1))
            temps = jnp.dot(high, bh_ref[...], preferred_element_type=F32)
            temps += jnp.dot(low, bh_ref[...], preferred_element_type=F32)
            temps += jnp.dot(high, bl_ref[...], preferred_element_type=F32)
            source = jnp.exp(0.5 * temps)
            layers = ab_ref[...] * source
            above = lax.broadcasted_iota(jnp.int32, (2 * levels, levels), 0) % levels
            level = lax.broadcasted_iota(jnp.int32, (2 * levels, levels), 1)
            upper = jnp.where(above < level, 1.0, 0.0).astype(BF16)
            overhead = jnp.dot(jnp.concatenate(split_pair(layers), axis=1), upper, preferred_element_type=F32)
            half = jnp.tanh(0.5 * layers)
            emitted = source * jnp.exp(-overhead) * (2.0 * half / (1.0 + half))
            high, low = split_pair(emitted)
            bright = jnp.dot(jnp.concatenate([high, low], axis=1), kh_ref[...], preferred_element_type=F32)
            bright += jnp.dot(high, kl_ref[...], preferred_element_type=F32)
            place = step * tile + lax.broadcasted_iota(jnp.int32, (tile, 1), 0)
            out_ref[0, side] = jnp.where(place < count_ref[0], bright, 0.0)

    def whole(array):
        return pl.BlockSpec(array.shape, lambda i, c: (0,) * array.ndim)

    def tiled(wide):
        return pl.BlockSpec((tile, wide), lambda i, c: (i, 0))

    constants = (basis_high, basis_low, absorb[None, :], kernel_twice, kernel_low)
    return pl.pallas_call(
        body,
        grid_spec=pltpu.PrefetchScalarGridSpec(
            num_scalar_prefetch=1,
            grid=(NLON // tile,),
            in_specs=[tiled(4 * columns), whole(spectra), tiled(depth), tiled(depth)]
            + [whole(array) for array in constants],
            out_specs=pl.BlockSpec((1, 2, tile, channels), lambda i, c: (0, 0, i, 0)),
            scratch_shapes=[pltpu.VMEM((depth, 2 * columns), BF16)],
        ),
        out_shape=jax.ShapeDtypeStruct((1, 2, NLON, channels), F32),
        compiler_params=pltpu.CompilerParams(vmem_limit_bytes=48 << 20),
        cost_estimate=pl.CostEstimate(flops=1, bytes_accessed=1, transcendentals=0),
        name="synthesize",
    )(row_counts, first_sums, spectra, *tables, *constants)


def move_legendre(spec, coefficients, legendre, row_counts, basis, absorb, peak_level, width):
    waves, _, own, columns = coefficients.shape
    held = legendre.shape[0]
    sources = spec // PLANES
    quarter = spec // 4
    me = lax.axis_index("spec").astype(jnp.int32)
    natural = jnp.transpose(coefficients, (0, 2, 1, 3)).reshape(waves * 2 * own, columns)

    def swap(value, distance, use=None):
        pairs = [(i, i ^ distance) for i in range(spec) if use is None or use(i)]
        return lax.ppermute(value, "spec", pairs)

    def after(values, earlier):
        return lax.optimization_barrier((values, earlier))[0]

    arranged = arrange_legendre(legendre, me, spec, waves)
    arrived = [lax.all_to_all(half, "spec", split_axis=0, concat_axis=0, tiled=True) for half in arranged]
    plane_waves = jnp.arange(waves, dtype=jnp.int32).reshape(PLANES, -1)
    tables = wave_tables(row_counts[0], (jnp.concatenate((plane_waves[:2].reshape(-1), plane_waves[3])), plane_waves[2]))
    kernel = split_constant(channel_kernel(peak_level, width, basis.shape[1]))
    couple = jnp.arange(spec // 2, dtype=jnp.int32) ^ (me >> 1)
    order = jnp.concatenate(((couple & 1) * quarter + (couple >> 1), (me & 1)[None]))

    def contract(plane, earlier):
        return partial_rows(after(order, earlier), arrived[0], natural, plane * sources, sources, 0, own)

    def add_cores(keep, other):
        return keep[quarter:] + other[quarter:], keep[:quarter] + other[:quarter]

    def between_planes(value, plane):
        use = lambda i: (plane * held + 2 * (i // sources) * own) * sources < waves
        return [swap(value[away], sources * away, use) for away in range(1, PLANES)]

    keep3, send3 = contract(3, (tables, kernel))
    keep0, send0 = contract(0, send3)
    keep1, send1 = contract(1, send0)
    both3 = (keep3 + swap(send3, 1)).reshape(2, quarter, *keep3.shape[1:])
    early = between_planes(jnp.swapaxes(both3, 0, 1), 3)
    side0, own0 = add_cores(keep0, swap(send0, 1))
    keep2, send2 = contract(2, (side0, both3, send1))
    sum0 = own0 + swap(side0, 2)
    side1, own1 = add_cores(keep1, swap(send1, 1))
    late0 = between_planes(after(sum0, early), 0)

    keep2, other2 = after((keep2, swap(send2, 1)), (sum0, side1))
    side2, own2 = add_cores(keep2, other2)
    sum1 = own1 + swap(side1, 2)
    late1 = between_planes(after(sum1, side2), 1)
    sum3 = both3[:, 0] + sum(early)
    sum3 = sum3[0] + swap(after(sum3[1], side2), 2)
    sum2 = own2 + swap(side2, 2)
    late2 = between_planes(after(sum2, (late0, late1, sum3)), 2)
    first_sums = fourier_sums(jnp.concatenate((sum0[0] + sum(late0), sum1[0] + sum(late1), sum3)), tables[:2])
    last = sum2[0] + sum(late2)
    return synthesize(row_counts, first_sums, last, tables[2:], basis, absorb, *kernel)


def solution(mesh):
    spec = mesh.shape["spec"]
    placed = (
        P("draws", None, "spec", None),
        P("spec", None, None, None),
        P("spec"),
        P(),
        P(),
        P(),
        P(),
    )

    def on_device(coefficients, legendre, *others):
        held, _, _, rows = legendre.shape
        own = coefficients.shape[2]
        if rows == spec and 8 * rows == LANES and held % (4 * HALVES) == 0 and rows <= own:
            return move_legendre(spec, coefficients, legendre, *others)
        return move_coefficients(coefficients, legendre, *others)

    return jax.shard_map(
        on_device,
        mesh=mesh,
        in_specs=placed,
        out_specs=P(("draws", "spec"), None, None, None),
        check_vma=False,
    )
```
